32 devices in a mesh: batch: 4 (over y, x), seq: 8 (over z, core).
Axes of the slice: x: 2, y: 2, z: 4, core: 2. Of those that a mesh axis runs over, the one named last changes fastest.
Arguments:
- query_source: bfloat16 [4, 2816, 4096], P('batch', 'seq'), may hold values from -6 to 6
- key_source: bfloat16 [4, 2816, 4096], P('batch', 'seq'), may hold values from -6 to 6
- value_source: bfloat16 [4, 2816, 4096], P('batch', 'seq'), may hold values from -6 to 6
- send_list: int32 [4, 8, 4, 32], P('batch', 'seq'), may hold values from 0 to 351, as said below
- slab_from: int32 [4, 2048], P('batch', 'seq'), may hold values from 0 to 479, as said below
- bounds: int32 [4, 16], P('batch'), may hold values from 0 to 1920, as said below
- filters: bfloat16 [4096, 128], replicated, may hold values from -0.5 to 0.5
- skip_gain: float32 [4096], replicated, may hold values from 0.5 to 2
- out_cotangent: bfloat16 [4, 2048, 4096], P('batch', 'seq'), may hold values from -6 to 6
Outputs:
- gated_output: bfloat16 [4, 2048, 4096], P('batch', 'seq')
- query_grad: bfloat16 [4, 2816, 4096], P('batch', 'seq')
- key_grad: bfloat16 [4, 2816, 4096], P('batch', 'seq')
- value_grad: bfloat16 [4, 2816, 4096], P('batch', 'seq')
- filter_grad: float32 [4096, 128], P('seq')
- skip_grad: float32 [4096], P('seq')
The draws below stay inside these ranges and needn't reach their ends.
Inputs may be any that keep to these rules, and one draw needn't show every extreme that they name: For source (e, s) and destination batch index d, the first n entries of send_list[e, s, d] are distinct source rows of (e, s) that go to (d, s), with n between 0 and 32, n = 0 for d = e, and n = 32 for some pair at every s; the remaining entries are 0. No source row is listed twice, and no listed row is also kept by its own device. `slab_from`: the 256 entries of one device name, in no set order, its kept own source rows (values below 352) and every row listed to it: value 352 + e * 32 + m for the m-th listed row from source e; each exactly once. bounds[b, 0] = 0 and the starts rise by 128 or more; the last is at most 1920.
All inputs are finite; a program needn't handle non-finite values.
Results may differ from the reference program's by a relative error of at most 0.0075.
Values may be sent and summed in bfloat16 or wider, within the bound.
A program may use at most 192 MiB of HBM per device.

```python
import math
import jax
import jax.numpy as jnp
from jax import lax

CHANNELS = 4096
TAPS = 128
SPAN = 128
RECS = 16
MOVE = 32
ROWS = 256
SRC = 352
BATCHES = 4
SHARDS = 8
LENGTH = 2048
TOKENS = 8192


def routing_plan(key):
    base_key = jax.random.fold_in(key, 7001)
    split_keys = jax.random.split(base_key, 5)
    counts = jax.random.randint(split_keys[0], (SHARDS, BATCHES, BATCHES), MOVE // 2, MOVE + 1)
    chosen_step = jax.random.randint(split_keys[2], (SHARDS,), 1, BATCHES)
    chosen_src = jnp.full((SHARDS,), BATCHES - 1, jnp.int32)
    chosen_dest = (chosen_src + chosen_step) % BATCHES
    dest_ids = jnp.arange(BATCHES, dtype=jnp.int32)[None, :, None]
    src_ids = jnp.arange(BATCHES, dtype=jnp.int32)[None, None, :]
    is_full = (dest_ids == chosen_dest[:, None, None]) & (src_ids == chosen_src[:, None, None])
    counts = jnp.where(is_full, MOVE, counts)
    counts = jnp.where(dest_ids == src_ids, 0, counts).astype(jnp.int32)
    kept_rows = ROWS - jnp.sum(counts, axis=2)

    def shuffled(one_key, count):
        return jax.random.permutation(one_key, count).astype(jnp.int32)
    outgoing = jnp.transpose(counts, (0, 2, 1))
    before = jnp.cumsum(outgoing, axis=2) - outgoing
    first_slot = kept_rows[:, :, None] + before
    device_keys = jax.random.split(split_keys[3], SHARDS * BATCHES)
    orders = jax.vmap(lambda one_key: shuffled(one_key, SRC))(device_keys).reshape(SHARDS, BATCHES, SRC)
    target_slot = jnp.take_along_axis(first_slot, jnp.broadcast_to(chosen_dest[:, None, None], (SHARDS, BATCHES, 1)), axis=2)
    positions = jnp.arange(SRC, dtype=jnp.int32)[None, None, :]
    top_place = jnp.sum(jnp.where(orders == SRC - 1, positions, 0), axis=2, keepdims=True)
    target_value = jnp.take_along_axis(orders, target_slot, axis=2)
    orders = jnp.where(positions == target_slot, SRC - 1, jnp.where(positions == top_place, target_value, orders)).astype(jnp.int32)
    lanes = jnp.arange(MOVE, dtype=jnp.int32)
    slots = jnp.minimum(first_slot[..., None] + lanes, SRC - 1)
    named_rows = jnp.take_along_axis(orders, slots.reshape(SHARDS, BATCHES, BATCHES * MOVE), axis=2)
    named_rows = named_rows.reshape(SHARDS, BATCHES, BATCHES, MOVE)
    is_valid = lanes[None, None, None, :] < outgoing[..., None]
    send_rows = jnp.where(is_valid, named_rows, 0)
    send_rows = jnp.transpose(send_rows, (1, 0, 2, 3)).astype(jnp.int32)
    own_valid = jnp.arange(ROWS, dtype=jnp.int32)[None, None, :] < kept_rows[:, :, None]
    own_values = orders[:, :, :ROWS]
    import_values = jnp.broadcast_to(SRC + jnp.arange(BATCHES * MOVE, dtype=jnp.int32), (SHARDS, BATCHES, BATCHES * MOVE))
    import_valid = (lanes[None, None, None, :] < counts[..., None]).reshape(SHARDS, BATCHES, BATCHES * MOVE)
    candidates = jnp.concatenate([own_values, import_values], axis=2)
    valid_all = jnp.concatenate([own_valid, import_valid], axis=2)
    total_width = ROWS + BATCHES * MOVE
    score_keys = jax.random.split(split_keys[4], SHARDS * BATCHES)
    scores = jax.vmap(lambda one_key: shuffled(one_key, total_width))(score_keys).reshape(SHARDS, BATCHES, total_width)
    scores = scores + jnp.where(valid_all, 0, total_width)
    ranked = jnp.argsort(scores, axis=2, stable=True)[:, :, :ROWS]
    picked = jnp.take_along_axis(candidates, ranked, axis=2)
    slab_rows = jnp.transpose(picked, (1, 0, 2)).reshape(BATCHES, SHARDS * ROWS).astype(jnp.int32)
    return (send_rows, slab_rows)


def draw_send_list(key, part):
    return routing_plan(key)[0]


def draw_slab_from(key, part):
    return routing_plan(key)[1]


def draw_bounds(key, part):
    base_key = jax.random.fold_in(key, 7002)
    spare_rows = LENGTH - RECS * TAPS
    row_keys = jax.random.split(base_key, BATCHES)

    def draw_row(row_key):
        cut_points = jnp.sort(jax.random.permutation(row_key, spare_rows + RECS - 1)[:RECS - 1]).astype(jnp.int32)
        edges = jnp.concatenate([jnp.array([-1], jnp.int32), cut_points, jnp.array([spare_rows + RECS - 1], jnp.int32)])
        extra_gaps = edges[1:] - edges[:-1] - 1
        lengths = TAPS + extra_gaps
        return (jnp.cumsum(lengths) - lengths).astype(jnp.int32)
    return jax.vmap(draw_row)(row_keys)


def raised(drawn, stream_key, source, target, shards_of, factor):
    def block_of(axis_at):
        return (jnp.arange(drawn.shape[axis_at]) // (drawn.shape[axis_at] // shards_of)).reshape((-1,) + (1,) * (drawn.ndim - 1 - axis_at))

    near = jax.random.permutation(stream_key, shards_of)[block_of(target)]
    far = (block_of(target) + shards_of // 2) % shards_of
    return jnp.where((block_of(source) == near) | (block_of(source) == far), factor * drawn, drawn)


def steps_of(key, shape, cuts, low, high):
    def one(dim, parts):
        draws = jax.random.uniform(jax.random.fold_in(jax.random.fold_in(key, 6), dim), (parts,), jnp.float32, low / len(cuts), high / len(cuts))
        return jnp.repeat(jnp.exp(draws), shape[dim] // parts).reshape((-1,) + (1,) * (len(shape) - dim - 1))

    level = one(*cuts[0])
    for cut in cuts[1:]:
        level = level * one(*cut)
    return level


def noise(own_key, dims, deviation, limit, shards=(), kind=jnp.bfloat16):
    factor_of = steps_of(own_key, dims, shards, -0.22, 0.18) if shards else 1.0
    drawn = jax.random.normal(own_key, dims, jnp.float32) * deviation * factor_of
    return jnp.minimum(jnp.maximum(drawn, -limit), limit).astype(kind)


def bell_draw_with(key, dims, spread, reach, pieces, heavy, held_as=jnp.bfloat16):
    drawn = spread * jax.random.normal(key, dims, jnp.float32)
    if pieces:
        drawn = drawn * steps_of(key, dims, pieces, -0.22, 0.18)
    return jnp.clip(raised(drawn, jax.random.fold_in(key, 3), *heavy), -reach, reach).astype(held_as)


def setup_inputs(seed: int = 0) -> dict:
    arg_keys = jax.random.split(jax.random.key(seed), 10)
    query_source = noise(arg_keys[0], (BATCHES, SHARDS * SRC, CHANNELS), 1.0, 6.0, ((0, 4), (1, 8)))
    key_source = noise(arg_keys[1], (BATCHES, SHARDS * SRC, CHANNELS), 1.0, 6.0, ((0, 4), (1, 8)))
    value_source = noise(arg_keys[2], (BATCHES, SHARDS * SRC, CHANNELS), 1.0, 6.0, ((0, 4), (1, 8)))
    send_list = draw_send_list(jax.random.fold_in(arg_keys[9], 71), 0)
    slab_from = draw_slab_from(jax.random.fold_in(arg_keys[9], 71), 0)
    bounds = draw_bounds(jax.random.fold_in(arg_keys[9], 71), 0)
    filters = noise(arg_keys[6], (CHANNELS, TAPS), TAPS ** -0.5, 0.5)
    skip_gain = jnp.clip(jnp.exp(jax.random.uniform(arg_keys[7], (CHANNELS,), jnp.float32, math.log(0.5), math.log(2.0))), 0.5, 2.0)
    out_cotangent = bell_draw_with(arg_keys[8], (BATCHES, SHARDS * ROWS, CHANNELS), 1.0, 6.0, ((0, 4), (1, 8)), (1, 2, 8, 2.0))
    return {"query_source": query_source, "key_source": key_source, "value_source": value_source, "send_list": send_list, "slab_from": slab_from, "bounds": bounds, "filters": filters, "skip_gain": skip_gain, "out_cotangent": out_cotangent}


def record_parity(starts, places):
    counted = jnp.sum((starts[None, :] <= places[:, None]).astype(jnp.int32), axis=1)
    return (counted - 1) % 2


def reference(query_source, key_source, value_source, send_list, slab_from, bounds, filters, skip_gain, out_cotangent):
    slot_ids = slab_from.reshape(BATCHES, SHARDS, ROWS)
    is_own = slot_ids < SRC
    remote = jnp.maximum(slot_ids - SRC, 0)
    from_batch = remote // MOVE
    lane_ids = remote % MOVE
    shard_ids = jnp.arange(SHARDS, dtype=jnp.int32)[None, :, None]
    dest_ids = jnp.arange(BATCHES, dtype=jnp.int32)[:, None, None]
    remote_row = send_list[from_batch, shard_ids, dest_ids, lane_ids]
    owner_batch = jnp.where(is_own, dest_ids, from_batch)
    source_row = jnp.where(is_own, slot_ids, remote_row)
    flat_index = ((owner_batch * SHARDS + shard_ids) * SRC + source_row).reshape(BATCHES, SHARDS * ROWS).astype(jnp.int32)

    natural = jnp.arange(LENGTH, dtype=jnp.int32)
    span_of = natural // SPAN
    in_first = span_of < SHARDS
    block_ids = jnp.where(in_first, span_of, 2 * SHARDS - 1 - span_of)
    storage_index = block_ids * ROWS + jnp.where(in_first, 0, SPAN) + natural % SPAN
    stored = jnp.arange(SHARDS * ROWS, dtype=jnp.int32)
    home_block = stored // ROWS
    within = stored % ROWS
    natural_index = jnp.where(within < SPAN, home_block * SPAN + within, (2 * SHARDS - 1 - home_block) * SPAN + within - SPAN)
    take_index = flat_index[:, storage_index]

    query_nat = query_source.reshape(-1, CHANNELS)[take_index]
    key_nat = key_source.reshape(-1, CHANNELS)[take_index]
    value_nat = value_source.reshape(-1, CHANNELS)[take_index]
    grad_nat = out_cotangent[:, storage_index]

    fft_length = 2 * LENGTH
    spectrum_taps = jnp.fft.rfft(jnp.transpose(filters.astype(jnp.float32)), fft_length, axis=0)

    def process_row(operands):
        query_row, key_row, value_row, grad_row, starts = operands
        query_float = query_row.astype(jnp.float32)
        key_float = key_row.astype(jnp.float32)
        value_float = value_row.astype(jnp.float32)
        mixed = lax.optimization_barrier((key_float * value_float).astype(jnp.bfloat16)).astype(jnp.float32)
        parity = record_parity(starts, jnp.arange(LENGTH, dtype=jnp.int32))
        filtered = skip_gain[None, :] * mixed
        spectra = []
        for parity_value in (0, 1):
            selector = (parity == parity_value).astype(jnp.float32)[:, None]
            spectrum = jnp.fft.rfft(mixed * selector, fft_length, axis=0)
            spectra.append((selector, spectrum))
            filtered = filtered + selector * jnp.fft.irfft(spectrum * spectrum_taps, fft_length, axis=0)[:LENGTH]
        output_row = (query_float * filtered).astype(jnp.bfloat16)
        grad_float = grad_row.astype(jnp.float32)
        gated = lax.optimization_barrier((grad_float * query_float).astype(jnp.bfloat16)).astype(jnp.float32)
        query_grad_row = (grad_float * filtered).astype(jnp.bfloat16)
        grad_mixed = skip_gain[None, :] * gated
        grad_weights = jnp.zeros((TAPS, CHANNELS), jnp.float32)
        for selector, spectrum in spectra:
            spectrum_grad = jnp.fft.rfft(gated * selector, fft_length, axis=0)
            grad_mixed = grad_mixed + selector * jnp.fft.irfft(spectrum_grad * jnp.conj(spectrum_taps), fft_length, axis=0)[:LENGTH]
            grad_weights = grad_weights + jnp.fft.irfft(spectrum_grad * jnp.conj(spectrum), fft_length, axis=0)[:TAPS]
        key_grad_row = (grad_mixed * value_float).astype(jnp.bfloat16)
        value_grad_row = (grad_mixed * key_float).astype(jnp.bfloat16)
        skip_row = jnp.sum(gated * mixed, axis=0)
        return output_row, query_grad_row, key_grad_row, value_grad_row, jnp.transpose(grad_weights), skip_row

    results = lax.map(process_row, (query_nat, key_nat, value_nat, grad_nat, bounds))
    output_nat, query_gnat, key_gnat, value_gnat, weight_rows, skip_rows = results
    gated_output = output_nat[:, natural_index]

    def to_source(grad_natural):
        slab_grad = grad_natural[:, natural_index].reshape(-1, CHANNELS)
        zeroed = jnp.zeros((BATCHES * SHARDS * SRC, CHANNELS), jnp.bfloat16)
        return zeroed.at[flat_index.reshape(-1)].set(slab_grad).reshape(BATCHES, SHARDS * SRC, CHANNELS)

    factor = float(TOKENS) ** -0.5
    filter_grad = jnp.sum(weight_rows, axis=0) * factor
    skip_grad = jnp.sum(skip_rows, axis=0) * factor
    return gated_output, to_source(query_gnat), to_source(key_gnat), to_source(value_gnat), filter_grad, skip_grad
```

```python
import functools

import jax
import jax.numpy as jnp
import numpy as np
from jax import lax
from jax.experimental import pallas as pl
from jax.experimental.pallas import tpu as pltpu
from jax.sharding import PartitionSpec as P

CHANNELS = 4096
TAPS = 128
SPAN = 128
MOVE = 32
ROWS = 256
WINDOW = 2 * SPAN
EXTRA = 8
GROUPS = 2

F32 = jnp.float32
BF16 = jnp.bfloat16


def waves(places):
    angles = 2.0 * np.pi / WINDOW * np.outer(np.arange(SPAN) + 0.5, places)
    return np.cos(angles), np.sin(angles)


def forward_waves(places):
    cos, sin = waves(places)
    return np.concatenate([cos, -sin], axis=0).astype(np.float32)


def inverse_waves(places):
    cos, sin = waves(places)
    return (np.concatenate([cos, -sin], axis=0).T / SPAN).astype(np.float32)


def dot(a, b):
    return jnp.dot(a, b, preferred_element_type=F32)


def times(a, b):
    return (a.astype(F32) * b.astype(F32)).astype(BF16)


def pack_kernel(routes, query, key, value, sent):
    batches = sent.shape[0]
    width = sent.shape[2]
    picked_query = dot(routes[...], query[...]).astype(BF16)
    picked_mixed = dot(routes[...], times(key[...], value[...])).astype(BF16)
    sent[:, :MOVE, :] = picked_query.reshape(batches, MOVE, width)
    sent[:, MOVE:, :] = picked_mixed.reshape(batches, MOVE, width)


def slab_kernel(own_hot, far_hot, query, key, value, arrived, cotangent, query_slab, right, left):
    width = query.shape[1]
    far_query = arrived[:, :MOVE, :].reshape(-1, width)
    far_mixed = arrived[:, MOVE:, :].reshape(-1, width)
    queries = (dot(own_hot[...], query[...]) + dot(far_hot[...], far_query)).astype(BF16)
    mixed = (
        dot(own_hot[...], times(key[...], value[...])) + dot(far_hot[...], far_mixed)
    ).astype(BF16)
    gated = times(cotangent[...], queries)
    query_slab[...] = queries
    right[:SPAN, :] = mixed[:SPAN]
    right[SPAN:, :] = gated[SPAN:]
    left[:SPAN, :] = mixed[SPAN:]
    left[SPAN:, :] = gated[:SPAN]


def main_kernel(
    flag,
    wave_in,
    wave_gate,
    wave_ahead,
    wave_taps,
    wave_out,
    wave_grad,
    wave_weights,
    far_back,
    filters,
    skip_gain,
    query_slab,
    right,
    left,
    from_left,
    from_right,
    cotangent,
    *rest,
):
    out, grad_query, grad_mixed, sent, sums = rest[-5:]
    width = query_slab.shape[1]
    batches = sent.shape[0]
    last = flag[0] == 1
    taps = lax.dot_general(
        wave_taps[...], filters[...], (((1,), (1,)), ((), ())), preferred_element_type=F32
    )
    tap_re, tap_im = taps[:SPAN], taps[SPAN:]
    gain = skip_gain[...]
    mixed = (right[:SPAN, :], left[:SPAN, :])
    gated = (left[SPAN:, :], right[SPAN:, :])
    before = (from_left[:SPAN, :], jnp.where(last, mixed[0], from_right[:SPAN, :]))
    ahead = (jnp.where(last, gated[1], from_right[SPAN:, :]), from_left[SPAN:, :])
    weight_re = jnp.zeros((SPAN, width), F32)
    weight_im = jnp.zeros((SPAN, width), F32)
    skip_sum = jnp.zeros((1, width), F32)
    query_parts, mixed_parts = [], []
    for block in range(2):
        rows = slice(block * SPAN, (block + 1) * SPAN)
        spec = dot(wave_in[block], jnp.concatenate([before[block], mixed[block]], axis=0))
        gate = dot(wave_gate[block], gated[block])
        both = gate + dot(wave_ahead[block], ahead[block])
        prods, backs = [], []
        for parity in range(2):
            re = slice(2 * parity * SPAN, (2 * parity + 1) * SPAN)
            im = slice((2 * parity + 1) * SPAN, (2 * parity + 2) * SPAN)
            x_re, x_im = spec[re], spec[im]
            g_re, g_im = gate[re], gate[im]
            b_re, b_im = both[re], both[im]
            prods += [
                (tap_re * x_re - tap_im * x_im).astype(BF16),
                (tap_re * x_im + tap_im * x_re).astype(BF16),
            ]
            backs += [
                (tap_re * b_re + tap_im * b_im).astype(BF16),
                (tap_re * b_im - tap_im * b_re).astype(BF16),
            ]
            weight_re += g_re * x_re + g_im * x_im
            weight_im += g_re * x_im - g_im * x_re
        mixed_float = mixed[block].astype(F32)
        gated_float = gated[block].astype(F32)
        filtered = dot(wave_out[block], jnp.concatenate(prods, axis=0)) + gain * mixed_float
        back = dot(wave_grad[block], jnp.concatenate(backs, axis=0)) + gain * gated_float
        out[rows, :] = (query_slab[rows, :].astype(F32) * filtered).astype(BF16)
        query_parts.append((cotangent[rows, :].astype(F32) * filtered).astype(BF16))
        mixed_parts.append(back.astype(BF16))
        grad_query[rows, :] = query_parts[-1]
        grad_mixed[rows, :] = mixed_parts[-1]
        skip_sum += jnp.sum(gated_float * mixed_float, axis=0, keepdims=True)
    far_query = dot(far_back[...], jnp.concatenate(query_parts, axis=0)).astype(BF16)
    far_mixed = dot(far_back[...], jnp.concatenate(mixed_parts, axis=0)).astype(BF16)
    sent[:, :MOVE, :] = far_query.reshape(batches, MOVE, width)
    sent[:, MOVE:, :] = far_mixed.reshape(batches, MOVE, width)
    weights = jnp.concatenate([weight_re, weight_im], axis=0)
    sums[:TAPS, :] = dot(wave_weights[...], weights.astype(BF16))
    sums[TAPS:, :] = jnp.broadcast_to(skip_sum, (EXTRA, width))


def settle_kernel(own_back, routes_back, slab_query, slab_mixed, arrived, key, value, *rest):
    query_grad, key_grad, value_grad = rest[-3:]
    width = key.shape[1]
    far_query = arrived[:, :MOVE, :].reshape(-1, width)
    far_mixed = arrived[:, MOVE:, :].reshape(-1, width)
    query_grad[...] = (
        dot(own_back[...], slab_query[...]) + dot(routes_back[...], far_query)
    ).astype(BF16)
    mixed = dot(own_back[...], slab_mixed[...]) + dot(routes_back[...], far_mixed)
    key_grad[...] = (mixed * value[...].astype(F32)).astype(BF16)
    value_grad[...] = (mixed * key[...].astype(F32)).astype(BF16)


def whole(shape):
    return pl.BlockSpec(shape, lambda i: (0,) * len(shape))


def cost(flops, moved):
    return pl.CostEstimate(flops=int(flops), bytes_accessed=int(moved), transcendentals=0)


def params():
    return pltpu.CompilerParams(vmem_limit_bytes=40 * 1024 * 1024)


def on_device(
    query_source,
    key_source,
    value_source,
    send_list,
    slab_from,
    bounds,
    filters,
    skip_gain,
    out_cotangent,
):
    shards = lax.axis_size("seq")
    batches = lax.axis_size("batch")
    shard_index = lax.axis_index("seq")
    query = query_source[0]
    key = key_source[0]
    value = value_source[0]
    cotangent = out_cotangent[0]
    routes = send_list[0, 0].reshape(-1)
    picks = slab_from[0]
    starts = bounds[0]
    source_rows = query.shape[0]
    far_rows = batches * MOVE
    length = shards * ROWS
    piece = CHANNELS // shards
    width = min(256, piece)
    splits = piece // width
    steps = shards // GROUPS
    part = steps * width

    own_ids = jnp.arange(source_rows, dtype=jnp.int32)
    far_ids = source_rows + jnp.arange(far_rows, dtype=jnp.int32)
    routes_hot = (routes[:, None] == own_ids[None, :]).astype(BF16)
    routes_back = (own_ids[:, None] == routes[None, :]).astype(BF16)
    own_hot = (picks[:, None] == own_ids[None, :]).astype(BF16)
    far_hot = (picks[:, None] == far_ids[None, :]).astype(BF16)
    own_back = (own_ids[:, None] == picks[None, :]).astype(BF16)
    far_back = (far_ids[:, None] == picks[None, :]).astype(BF16)

    span_ids = jnp.stack([shard_index, 2 * shards - 1 - shard_index])
    places = (span_ids[:, None] - 1) * SPAN + jnp.arange(3 * SPAN, dtype=jnp.int32)[None, :]
    counted = jnp.sum((starts[None, None, :] <= places[:, :, None]).astype(jnp.int32), axis=2)
    inside = (places >= 0) & (places < length)
    parity = (counted - 1) % 2
    masks = jnp.stack(
        [(inside & (parity == 0)), (inside & (parity == 1))], axis=1
    ).astype(F32)

    def masked_in(matrix, mask):
        return (matrix[None, None] * mask[:, :, None, :]).reshape(2, 4 * SPAN, -1).astype(BF16)

    def masked_out(matrix, mask):
        wide = matrix[None, :, None, :] * jnp.swapaxes(mask, 1, 2)[:, :, :, None]
        return wide.reshape(2, SPAN, 4 * SPAN).astype(BF16)

    near, far = np.arange(SPAN), SPAN + np.arange(SPAN)
    wave_in = masked_in(forward_waves(np.arange(WINDOW)), masks[:, :, :WINDOW])
    wave_gate = masked_in(forward_waves(near), masks[:, :, SPAN:WINDOW])
    wave_ahead = masked_in(forward_waves(far), masks[:, :, WINDOW:])
    wave_taps = jnp.asarray(forward_waves(near), BF16)
    wave_out = masked_out(inverse_waves(far), masks[:, :, SPAN:WINDOW])
    wave_grad = masked_out(inverse_waves(near), masks[:, :, SPAN:WINDOW])
    wave_weights = jnp.asarray(inverse_waves(SPAN - np.arange(TAPS)), BF16)
    flag = (shard_index == shards - 1).astype(jnp.int32).reshape(1)
    gain = skip_gain.reshape(1, CHANNELS)

    def place(split, group):
        return lambda i: (group * steps + i) * splits + split

    chunks = [(split, group) for split in range(splits) for group in range(GROUPS)]
    right_way = [(i, i + 1) for i in range(shards - 1)]
    left_way = [(i + 1, i) for i in range(shards - 1)]

    def part_spec(rows):
        return pl.BlockSpec((rows, width), lambda i: (0, i))

    sent_spec = pl.BlockSpec((batches, 2 * MOVE, width), lambda i: (0, 0, i))
    sent_shape = jax.ShapeDtypeStruct((batches, 2 * MOVE, part), BF16)
    slab_shape = jax.ShapeDtypeStruct((ROWS, part), BF16)
    any_spec = pl.BlockSpec(memory_space=pl.ANY)

    arrived = {}
    for chunk in chunks:
        at = place(*chunk)
        full = lambda rows: pl.BlockSpec((rows, width), lambda i: (0, at(i)))
        sent = pl.pallas_call(
            pack_kernel,
            grid=(steps,),
            in_specs=[whole((far_rows, source_rows))] + [full(source_rows)] * 3,
            out_specs=sent_spec,
            out_shape=sent_shape,
            compiler_params=params(),
            cost_estimate=cost(4 * far_rows * source_rows * part, 8 * source_rows * part),
        )(routes_hot, query, key, value)
        arrived[chunk] = lax.all_to_all(sent, "batch", split_axis=0, concat_axis=0, tiled=True)

    slabs = {}
    for chunk in chunks:
        at = place(*chunk)
        full = lambda rows: pl.BlockSpec((rows, width), lambda i: (0, at(i)))
        query_slab, right, left = pl.pallas_call(
            slab_kernel,
            grid=(steps,),
            in_specs=[whole((ROWS, source_rows)), whole((ROWS, far_rows))]
            + [full(source_rows)] * 3
            + [sent_spec, full(ROWS)],
            out_specs=[part_spec(ROWS)] * 3,
            out_shape=[slab_shape] * 3,
            compiler_params=params(),
            cost_estimate=cost(4 * ROWS * 480 * part, 12 * source_rows * part),
        )(own_hot, far_hot, query, key, value, arrived[chunk], cotangent)
        from_left = lax.ppermute(right, "seq", right_way)
        from_right = lax.ppermute(left, "seq", left_way)
        slabs[chunk] = (query_slab, right, left, from_left, from_right)

    out = None
    grads = {}
    for chunk in chunks:
        at = place(*chunk)
        full = lambda rows: pl.BlockSpec((rows, width), lambda i: (0, at(i)))
        carried = [] if out is None else [out]
        operands = [
            flag,
            wave_in,
            wave_gate,
            wave_ahead,
            wave_taps,
            wave_out,
            wave_grad,
            wave_weights,
            far_back,
        ]
        in_specs = [pl.BlockSpec(memory_space=pltpu.SMEM)]
        in_specs += [whole(operand.shape) for operand in operands[1:]]
        in_specs += [
            pl.BlockSpec((width, TAPS), lambda i: (at(i), 0)),
            full(1),
        ]
        in_specs += [part_spec(ROWS)] * 5 + [full(ROWS)]
        operands += [filters, gain, *slabs[chunk], cotangent]
        aliases = {len(operands): 0} if carried else {}
        out, slab_query, slab_mixed, sent, sums = pl.pallas_call(
            main_kernel,
            grid=(steps,),
            in_specs=in_specs + [any_spec] * len(carried),
            out_specs=[full(ROWS), part_spec(ROWS), part_spec(ROWS), sent_spec, part_spec(TAPS + EXTRA)],
            out_shape=[
                jax.ShapeDtypeStruct((ROWS, CHANNELS), BF16),
                slab_shape,
                slab_shape,
                sent_shape,
                jax.ShapeDtypeStruct((TAPS + EXTRA, part), F32),
            ],
            input_output_aliases=aliases,
            compiler_params=params(),
            cost_estimate=cost(3000 * 1024 * part, 30 * ROWS * part),
        )(*operands, *carried)
        back = lax.all_to_all(sent, "batch", split_axis=0, concat_axis=0, tiled=True)
        grads[chunk] = (slab_query, slab_mixed, back, sums)

    totals = []
    for split in range(splits):
        joined = jnp.concatenate([grads[split, group][3] for group in range(GROUPS)], axis=1)
        shared = lax.psum_scatter(joined, "seq", scatter_dimension=1, tiled=True)
        totals.append(lax.psum(shared, "batch"))
    total = jnp.concatenate(totals, axis=1)

    results = []
    for chunk in chunks:
        at = place(*chunk)
        full = lambda rows: pl.BlockSpec((rows, width), lambda i: (0, at(i)))
        operands = [own_back, routes_back, *grads[chunk][:3], key, value]
        results = pl.pallas_call(
            settle_kernel,
            grid=(steps,),
            in_specs=[whole((source_rows, ROWS)), whole((source_rows, far_rows))]
            + [part_spec(ROWS)] * 2
            + [sent_spec]
            + [full(source_rows)] * 2
            + [any_spec] * len(results),
            out_specs=[full(source_rows)] * 3,
            out_shape=[jax.ShapeDtypeStruct((source_rows, CHANNELS), BF16)] * 3,
            input_output_aliases={len(operands) + n: n for n in range(len(results))},
            compiler_params=params(),
            cost_estimate=cost(4 * 480 * ROWS * part, 14 * source_rows * part),
        )(*operands, *results)
    factor = float(batches * shards * ROWS) ** (-0.5)
    return (
        out[None],
        results[0][None],
        results[1][None],
        results[2][None],
        jnp.transpose(total[:TAPS]) * factor,
        total[TAPS] * factor,
    )


def solution(mesh):
    return jax.shard_map(
        on_device,
        mesh=mesh,
        in_specs=(
            P("batch", "seq", None),
            P("batch", "seq", None),
            P("batch", "seq", None),
            P("batch", "seq", None, None),
            P("batch", "seq"),
            P("batch", None),
            P(),
            P(),
            P("batch", "seq", None),
        ),
        out_specs=(
            P("batch", "seq", None),
            P("batch", "seq", None),
            P("batch", "seq", None),
            P("batch", "seq", None),
            P("seq", None),
            P("seq"),
        ),
        check_vma=False,
    )
```

```python
import functools

import jax
import jax.numpy as jnp
import numpy as np
from jax import lax
from jax.experimental import pallas as pl
from jax.experimental.pallas import tpu as pltpu
from jax.sharding import PartitionSpec as P

CHANNELS = 4096
TAPS = 128
SPAN = 128
MOVE = 32
ROWS = 256
WINDOW = 2 * SPAN
EXTRA = 8

F32 = jnp.float32
BF16 = jnp.bfloat16


def waves(places):
    angles = 2.0 * np.pi / WINDOW * np.outer(np.arange(SPAN) + 0.5, places)
    return np.cos(angles), np.sin(angles)


def forward_waves(places):
    cos, sin = waves(places)
    return np.concatenate([cos, -sin], axis=0).astype(np.float32)


def inverse_waves(places):
    cos, sin = waves(places)
    return (np.concatenate([cos, -sin], axis=0).T / SPAN).astype(np.float32)


def dot(a, b):
    return jnp.dot(a, b, preferred_element_type=F32)


def times(a, b):
    return (a.astype(F32) * b.astype(F32)).astype(BF16)


def pack_kernel(routes, query, key, value, sent):
    batches = sent.shape[0]
    width = sent.shape[2]
    picked_query = dot(routes[...], query[...]).astype(BF16)
    picked_mixed = dot(routes[...], times(key[...], value[...])).astype(BF16)
    sent[:, :MOVE, :] = picked_query.reshape(batches, MOVE, width)
    sent[:, MOVE:, :] = picked_mixed.reshape(batches, MOVE, width)


def slab_kernel(own_hot, far_hot, query, key, value, arrived, cotangent, query_slab, right, left):
    width = query.shape[1]
    far_query = arrived[:, :MOVE, :].reshape(-1, width)
    far_mixed = arrived[:, MOVE:, :].reshape(-1, width)
    queries = (dot(own_hot[...], query[...]) + dot(far_hot[...], far_query)).astype(BF16)
    mixed = (
        dot(own_hot[...], times(key[...], value[...])) + dot(far_hot[...], far_mixed)
    ).astype(BF16)
    gated = times(cotangent[...], queries)
    query_slab[...] = queries
    right[:SPAN, :] = mixed[:SPAN]
    right[SPAN:, :] = gated[SPAN:]
    left[:SPAN, :] = mixed[SPAN:]
    left[SPAN:, :] = gated[:SPAN]


def weights_kernel(flag, wave_in, wave_gate, wave_weights, right, left, from_left, from_right, sums):
    width = right.shape[1]
    last = flag[0] == 1
    mixed = (right[:SPAN, :], left[:SPAN, :])
    gated = (left[SPAN:, :], right[SPAN:, :])
    before = (from_left[:SPAN, :], jnp.where(last, mixed[0], from_right[:SPAN, :]))
    weight_re = jnp.zeros((SPAN, width), F32)
    weight_im = jnp.zeros((SPAN, width), F32)
    skip_sum = jnp.zeros((1, width), F32)
    for block in range(2):
        spec = dot(wave_in[block], jnp.concatenate([before[block], mixed[block]], axis=0))
        gate = dot(wave_gate[block], gated[block])
        for parity in range(2):
            re = slice(2 * parity * SPAN, (2 * parity + 1) * SPAN)
            im = slice((2 * parity + 1) * SPAN, (2 * parity + 2) * SPAN)
            weight_re += gate[re] * spec[re] + gate[im] * spec[im]
            weight_im += gate[re] * spec[im] - gate[im] * spec[re]
        skip_sum += jnp.sum(
            gated[block].astype(F32) * mixed[block].astype(F32), axis=0, keepdims=True
        )
    weights = jnp.concatenate([weight_re, weight_im], axis=0)
    sums[:TAPS, :] = dot(wave_weights[...], weights.astype(BF16))
    sums[TAPS:, :] = jnp.broadcast_to(skip_sum, (EXTRA, width))


def main_kernel(
    flag,
    wave_in,
    wave_both,
    wave_taps,
    wave_out,
    wave_grad,
    far_back,
    filters,
    skip_gain,
    query_slab,
    right,
    left,
    from_left,
    from_right,
    cotangent,
    *rest,
):
    out, grad_query, grad_mixed, sent = rest[-4:]
    width = query_slab.shape[1]
    batches = sent.shape[0]
    last = flag[0] == 1
    taps = lax.dot_general(
        wave_taps[...], filters[...], (((1,), (1,)), ((), ())), preferred_element_type=F32
    )
    tap_re, tap_im = taps[:SPAN], taps[SPAN:]
    gain = skip_gain[...]
    mixed = (right[:SPAN, :], left[:SPAN, :])
    gated = (left[SPAN:, :], right[SPAN:, :])
    before = (from_left[:SPAN, :], jnp.where(last, mixed[0], from_right[:SPAN, :]))
    ahead = (jnp.where(last, gated[1], from_right[SPAN:, :]), from_left[SPAN:, :])
    query_parts, mixed_parts = [], []
    for block in range(2):
        rows = slice(block * SPAN, (block + 1) * SPAN)
        spec = dot(wave_in[block], jnp.concatenate([before[block], mixed[block]], axis=0))
        both = dot(wave_both[block], jnp.concatenate([gated[block], ahead[block]], axis=0))
        prods, backs = [], []
        for parity in range(2):
            re = slice(2 * parity * SPAN, (2 * parity + 1) * SPAN)
            im = slice((2 * parity + 1) * SPAN, (2 * parity + 2) * SPAN)
            x_re, x_im = spec[re], spec[im]
            b_re, b_im = both[re], both[im]
            prods += [
                (tap_re * x_re - tap_im * x_im).astype(BF16),
                (tap_re * x_im + tap_im * x_re).astype(BF16),
            ]
            backs += [
                (tap_re * b_re + tap_im * b_im).astype(BF16),
                (tap_re * b_im - tap_im * b_re).astype(BF16),
            ]
        mixed_float = mixed[block].astype(F32)
        gated_float = gated[block].astype(F32)
        filtered = dot(wave_out[block], jnp.concatenate(prods, axis=0)) + gain * mixed_float
        back = dot(wave_grad[block], jnp.concatenate(backs, axis=0)) + gain * gated_float
        out[rows, :] = (query_slab[rows, :].astype(F32) * filtered).astype(BF16)
        query_parts.append((cotangent[rows, :].astype(F32) * filtered).astype(BF16))
        mixed_parts.append(back.astype(BF16))
        grad_query[rows, :] = query_parts[-1]
        grad_mixed[rows, :] = mixed_parts[-1]
    far_query = dot(far_back[...], jnp.concatenate(query_parts, axis=0)).astype(BF16)
    far_mixed = dot(far_back[...], jnp.concatenate(mixed_parts, axis=0)).astype(BF16)
    sent[:, :MOVE, :] = far_query.reshape(batches, MOVE, width)
    sent[:, MOVE:, :] = far_mixed.reshape(batches, MOVE, width)


def settle_kernel(own_back, routes_back, slab_query, slab_mixed, arrived, key, value, *rest):
    query_grad, key_grad, value_grad = rest[-3:]
    width = key.shape[1]
    far_query = arrived[:, :MOVE, :].reshape(-1, width)
    far_mixed = arrived[:, MOVE:, :].reshape(-1, width)
    query_grad[...] = (
        dot(own_back[...], slab_query[...]) + dot(routes_back[...], far_query)
    ).astype(BF16)
    mixed = dot(own_back[...], slab_mixed[...]) + dot(routes_back[...], far_mixed)
    key_grad[...] = (mixed * value[...].astype(F32)).astype(BF16)
    value_grad[...] = (mixed * key[...].astype(F32)).astype(BF16)


def whole(shape):
    return pl.BlockSpec(shape, lambda i: (0,) * len(shape))


def cost(flops, moved):
    return pl.CostEstimate(flops=int(flops), bytes_accessed=int(moved), transcendentals=0)


def params():
    return pltpu.CompilerParams(vmem_limit_bytes=60 * 1024 * 1024)


def on_device(
    query_source,
    key_source,
    value_source,
    send_list,
    slab_from,
    bounds,
    filters,
    skip_gain,
    out_cotangent,
):
    shards = lax.axis_size("seq")
    batches = lax.axis_size("batch")
    shard_index = lax.axis_index("seq")
    query = query_source[0]
    key = key_source[0]
    value = value_source[0]
    cotangent = out_cotangent[0]
    routes = send_list[0, 0].reshape(-1)
    picks = slab_from[0]
    starts = bounds[0]
    source_rows = query.shape[0]
    far_rows = batches * MOVE
    length = shards * ROWS
    piece = CHANNELS // shards
    width = 512
    splits = 2
    part = CHANNELS // splits
    steps = part // width

    own_ids = jnp.arange(source_rows, dtype=jnp.int32)
    far_ids = source_rows + jnp.arange(far_rows, dtype=jnp.int32)
    routes_hot = (routes[:, None] == own_ids[None, :]).astype(BF16)
    routes_back = (own_ids[:, None] == routes[None, :]).astype(BF16)
    own_hot = (picks[:, None] == own_ids[None, :]).astype(BF16)
    far_hot = (picks[:, None] == far_ids[None, :]).astype(BF16)
    own_back = (own_ids[:, None] == picks[None, :]).astype(BF16)
    far_back = (far_ids[:, None] == picks[None, :]).astype(BF16)

    span_ids = jnp.stack([shard_index, 2 * shards - 1 - shard_index])
    places = (span_ids[:, None] - 1) * SPAN + jnp.arange(3 * SPAN, dtype=jnp.int32)[None, :]
    counted = jnp.sum((starts[None, None, :] <= places[:, :, None]).astype(jnp.int32), axis=2)
    inside = (places >= 0) & (places < length)
    parity = (counted - 1) % 2
    masks = jnp.stack(
        [(inside & (parity == 0)), (inside & (parity == 1))], axis=1
    ).astype(F32)

    def masked_in(matrix, mask):
        return (matrix[None, None] * mask[:, :, None, :]).reshape(2, 4 * SPAN, -1).astype(BF16)

    def masked_out(matrix, mask):
        wide = matrix[None, :, None, :] * jnp.swapaxes(mask, 1, 2)[:, :, :, None]
        return wide.reshape(2, SPAN, 4 * SPAN).astype(BF16)

    near, far = np.arange(SPAN), SPAN + np.arange(SPAN)
    wave_in = masked_in(forward_waves(np.arange(WINDOW)), masks[:, :, :WINDOW])
    wave_gate = masked_in(forward_waves(near), masks[:, :, SPAN:WINDOW])
    wave_both = masked_in(forward_waves(np.arange(WINDOW)), masks[:, :, SPAN:])
    wave_taps = jnp.asarray(forward_waves(near), BF16)
    wave_out = masked_out(inverse_waves(far), masks[:, :, SPAN:WINDOW])
    wave_grad = masked_out(inverse_waves(near), masks[:, :, SPAN:WINDOW])
    wave_weights = jnp.asarray(inverse_waves(SPAN - np.arange(TAPS)), BF16)
    flag = (shard_index == shards - 1).astype(jnp.int32).reshape(1)
    gain = skip_gain.reshape(1, CHANNELS)

    def place(split):
        return lambda i: split * steps + i

    chunks = list(range(splits))
    right_way = [(i, i + 1) for i in range(shards - 1)]
    left_way = [(i + 1, i) for i in range(shards - 1)]

    def part_spec(rows):
        return pl.BlockSpec((rows, width), lambda i: (0, i))

    sent_spec = pl.BlockSpec((batches, 2 * MOVE, width), lambda i: (0, 0, i))
    sent_shape = jax.ShapeDtypeStruct((batches, 2 * MOVE, part), BF16)
    slab_shape = jax.ShapeDtypeStruct((ROWS, part), BF16)
    any_spec = pl.BlockSpec(memory_space=pl.ANY)

    arrived = {}
    for chunk in chunks:
        at = place(chunk)
        full = lambda rows: pl.BlockSpec((rows, width), lambda i: (0, at(i)))
        sent = pl.pallas_call(
            pack_kernel,
            grid=(steps,),
            in_specs=[whole((far_rows, source_rows))] + [full(source_rows)] * 3,
            out_specs=sent_spec,
            out_shape=sent_shape,
            compiler_params=params(),
            cost_estimate=cost(4 * far_rows * source_rows * part, 8 * source_rows * part),
        )(routes_hot, query, key, value)
        arrived[chunk] = lax.all_to_all(sent, "batch", split_axis=0, concat_axis=0, tiled=True)

    slabs = {}
    for chunk in chunks:
        at = place(chunk)
        full = lambda rows: pl.BlockSpec((rows, width), lambda i: (0, at(i)))
        query_slab, right, left = pl.pallas_call(
            slab_kernel,
            grid=(steps,),
            in_specs=[whole((ROWS, source_rows)), whole((ROWS, far_rows))]
            + [full(source_rows)] * 3
            + [sent_spec, full(ROWS)],
            out_specs=[part_spec(ROWS)] * 3,
            out_shape=[slab_shape] * 3,
            compiler_params=params(),
            cost_estimate=cost(4 * ROWS * 480 * part, 12 * source_rows * part),
        )(own_hot, far_hot, query, key, value, arrived[chunk], cotangent)
        from_left = lax.ppermute(right, "seq", right_way)
        from_right = lax.ppermute(left, "seq", left_way)
        slabs[chunk] = (query_slab, right, left, from_left, from_right)

    parts = []
    for chunk in chunks:
        operands = [flag, wave_in, wave_gate, wave_weights, *slabs[chunk][1:]]
        parts.append(
            pl.pallas_call(
                weights_kernel,
                grid=(steps,),
                in_specs=[pl.BlockSpec(memory_space=pltpu.SMEM)]
                + [whole(operand.shape) for operand in operands[1:4]]
                + [part_spec(ROWS)] * 4,
                out_specs=part_spec(TAPS + EXTRA),
                out_shape=jax.ShapeDtypeStruct((TAPS + EXTRA, part), F32),
                compiler_params=params(),
                cost_estimate=cost(1500 * 1024 * part, 12 * ROWS * part),
            )(*operands)
        )
    joined = jnp.concatenate(parts, axis=1).astype(BF16)
    pieces = jnp.swapaxes(joined.reshape(-1, shards, piece), 0, 1)
    met = lax.all_to_all(pieces, "seq", split_axis=0, concat_axis=0, tiled=True)
    summed = jnp.sum(met.astype(F32), axis=0).astype(BF16)
    copies = jnp.broadcast_to(summed[None], (batches, *summed.shape))
    shared = lax.all_to_all(copies, "batch", split_axis=0, concat_axis=0, tiled=True)
    total = jnp.sum(shared.astype(F32), axis=0)

    out = None
    grads = {}
    for chunk in chunks:
        at = place(chunk)
        full = lambda rows: pl.BlockSpec((rows, width), lambda i: (0, at(i)))
        carried = [] if out is None else [out]
        operands = [
            flag,
            wave_in,
            wave_both,
            wave_taps,
            wave_out,
            wave_grad,
            far_back,
        ]
        in_specs = [pl.BlockSpec(memory_space=pltpu.SMEM)]
        in_specs += [whole(operand.shape) for operand in operands[1:]]
        in_specs += [
            pl.BlockSpec((width, TAPS), lambda i: (at(i), 0)),
            full(1),
        ]
        in_specs += [part_spec(ROWS)] * 5 + [full(ROWS)]
        operands += [filters, gain, *slabs[chunk], cotangent]
        aliases = {len(operands): 0} if carried else {}
        out, slab_query, slab_mixed, sent = pl.pallas_call(
            main_kernel,
            grid=(steps,),
            in_specs=in_specs + [any_spec] * len(carried),
            out_specs=[full(ROWS), part_spec(ROWS), part_spec(ROWS), sent_spec],
            out_shape=[
                jax.ShapeDtypeStruct((ROWS, CHANNELS), BF16),
                slab_shape,
                slab_shape,
                sent_shape,
            ],
            input_output_aliases=aliases,
            compiler_params=params(),
            cost_estimate=cost(3000 * 1024 * part, 30 * ROWS * part),
        )(*operands, *carried)
        back = lax.all_to_all(sent, "batch", split_axis=0, concat_axis=0, tiled=True)
        grads[chunk] = (slab_query, slab_mixed, back)

    results = []
    for chunk in chunks:
        at = place(chunk)
        full = lambda rows: pl.BlockSpec((rows, width), lambda i: (0, at(i)))
        operands = [own_back, routes_back, *grads[chunk][:3], key, value]
        results = pl.pallas_call(
            settle_kernel,
            grid=(steps,),
            in_specs=[whole((source_rows, ROWS)), whole((source_rows, far_rows))]
            + [part_spec(ROWS)] * 2
            + [sent_spec]
            + [full(source_rows)] * 2
            + [any_spec] * len(results),
            out_specs=[full(source_rows)] * 3,
            out_shape=[jax.ShapeDtypeStruct((source_rows, CHANNELS), BF16)] * 3,
            input_output_aliases={len(operands) + n: n for n in range(len(results))},
            compiler_params=params(),
            cost_estimate=cost(4 * 480 * ROWS * part, 14 * source_rows * part),
        )(*operands, *results)
    factor = float(batches * shards * ROWS) ** (-0.5)
    return (
        out[None],
        results[0][None],
        results[1][None],
        results[2][None],
        jnp.transpose(total[:TAPS]) * factor,
        total[TAPS] * factor,
    )


def solution(mesh):
    return jax.shard_map(
        on_device,
        mesh=mesh,
        in_specs=(
            P("batch", "seq", None),
            P("batch", "seq", None),
            P("batch", "seq", None),
            P("batch", "seq", None, None),
            P("batch", "seq"),
            P("batch", None),
            P(),
            P(),
            P("batch", "seq", None),
        ),
        out_specs=(
            P("batch", "seq", None),
            P("batch", "seq", None),
            P("batch", "seq", None),
            P("batch", "seq", None),
            P("seq", None),
            P("seq"),
        ),
        check_vma=False,
    )
```
